32 devices in a mesh: pp: 4 (over y, core), ep: 8 (over z, x).
Axes of the slice: x: 2, y: 2, z: 4, core: 2. Of those that a mesh axis runs over, the one named last changes fastest.
Arguments:
- fwd_tokens: bfloat16 [4, 1024, 3584], P('pp', 'ep'), may hold values from -6 to 6
- fwd_routes: int32 [4, 1024, 2], P('pp', 'ep'), may hold values from 0 to 3, all different within a row; in each aligned block of 128 rows (0 to 127, 128 to 255, ..., all dimensions but the last counted through in order) at most 96 rows name the same one
- fwd_weights: float32 [4, 1024, 2], P('pp', 'ep'), may hold values from 0.2 to 1
- bwd_tokens: bfloat16 [4, 1024, 3584], P('pp', 'ep'), may hold values from -6 to 6
- bwd_grads: bfloat16 [4, 1024, 3584], P('pp', 'ep'), may hold values from -6 to 6
- bwd_routes: int32 [4, 1024, 2], P('pp', 'ep'), may hold values from 0 to 3, all different within a row; in each aligned block of 128 rows (0 to 127, 128 to 255, ..., all dimensions but the last counted through in order) at most 96 rows name the same one
- bwd_weights: float32 [4, 1024, 2], P('pp', 'ep'), may hold values from 0.2 to 1
- up_proj: bfloat16 [4, 3584, 4096], P('pp', None, 'ep'), may hold values from -0.09375 to 0.09375
- down_proj: bfloat16 [4, 4096, 3584], P('pp', 'ep'), may hold values from -0.1875 to 0.1875
Outputs:
- next_input: bfloat16 [4, 1024, 3584], P('pp', 'ep')
- prev_grad: bfloat16 [4, 1024, 3584], P('pp', 'ep')
The draws below stay inside these ranges and needn't reach their ends.
Inputs may be any that keep to these rules, and one draw needn't show every extreme that they name: `fwd_routes`: each row names 2 different experts. Among the 128 rows of one device no expert is named more than 96 times; on some devices some expert is named exactly 96 times. `bwd_routes`: as for fwd_routes.
All inputs are finite; a program needn't handle non-finite values.
Results may differ from the reference program's by a relative error of at most 0.0043.
Values may be sent and summed in bfloat16 or wider, within the bound.
A program may use at most 128 MiB of HBM per device.

```python
import math
import jax
import jax.numpy as jnp
import numpy as np
from jax import lax

D = 3584
FF_DEV = 512
TOP = 2
TOK_DEV = 128
FF = 1024
EXPERTS = 4
SECTIONS = 4
TOKENS = 1024
CAP = 96
N_EP = 8


def shard_levels(key, extent, pieces, low, top_value):
    def one(dim, blocks):
        draws = jax.random.uniform(jax.random.fold_in(jax.random.fold_in(key, 6), dim), (blocks,), jnp.float32, low / len(pieces), top_value / len(pieces))
        return jnp.repeat(jnp.exp(draws), extent[dim] // blocks).reshape((-1,) + (1,) * (len(extent) - dim - 1))

    level = one(*pieces[0])
    for cut in pieces[1:]:
        level = level * one(*cut)
    return level


def routed_block(key, own, number, rows, number_of, top, limit, slope):
    order = jax.random.permutation(key, number_of)
    packed, common = portions_of(number_of, rows * top, limit, slope, True), portions_of(number_of, rows * top, limit, slope, False)
    places = jnp.arange(number_of)

    def named(tallies, offset_by):
        used = int((tallies > 0).sum())
        fixed = max(1, used // 4)
        passed = fixed + (places - fixed + offset_by * (used - fixed)) % max(1, number_of - fixed)
        return jnp.zeros((number_of,), jnp.int32).at[order[jnp.where(places < fixed, places, passed)]].set(jnp.asarray(tallies, jnp.int32))

    tallies = jnp.where(number % 4 == 0, named(packed, number // 4), named(common, number - number // 4 - 1))
    mixed = jax.random.permutation(jax.random.fold_in(own, 3), number_of)
    donor, receiver = mixed[0:number_of // 2 * 2:2], mixed[1:number_of // 2 * 2:2]
    margin = jnp.minimum(tallies[donor] - 1, limit - tallies[receiver]) // 2
    margin = jnp.where((donor == order[0]) | (receiver == order[0]) | (tallies[receiver] == 0), 0, jnp.maximum(margin, 0))
    passed = jax.random.randint(jax.random.fold_in(own, 4), (number_of // 2,), 0, 1 << 20) % (margin + 1)
    tallies = tallies.at[donor].add(-passed).at[receiver].add(passed)
    members = jnp.searchsorted(jnp.cumsum(tallies), jnp.arange(rows * top), side="right").astype(jnp.int32)
    listing = members.reshape(top, rows).T
    listing = listing[jax.random.permutation(jax.random.fold_in(own, 1), rows)]
    offset_by = jax.random.randint(jax.random.fold_in(own, 2), (rows, 1), 0, top)
    return jnp.take_along_axis(listing, (jnp.arange(top)[None, :] + offset_by) % top, axis=1)


def portions_of(amount, total, limit, slope, full):
    loads = [(1 << 20) // math.isqrt(rank ** slope) + 1 for rank in range(1, amount + 1)]
    largest = limit if full else min(limit, max(-(-total // amount), total * loads[0] // sum(loads)))
    least = 1 if total - largest >= amount - 1 else 0
    holding, spare = [largest] + [least] * (amount - 1), total - largest - least * (amount - 1)
    while spare > 0:
        free = [i for i in range(1, amount) if holding[i] < largest] or [i for i in range(1, amount) if holding[i] < limit]
        mass, remaining = sum([loads[i] for i in free]), spare
        for i in free:
            more = min(limit - holding[i], max(1, remaining * loads[i] // mass), spare)
            holding[i] = holding[i] + more
            spare = spare - more
    return np.array(holding)


def bell_draw(rng, dims, width, reach, split=(), kind=jnp.bfloat16):
    entries = width * jax.random.normal(rng, dims, jnp.float32)
    if split:
        entries = entries * shard_levels(rng, dims, split, -0.22, 0.18)
    return jnp.clip(entries, -reach, reach).astype(kind)


def setup_inputs(seed: int = 0) -> dict:
    streams_of = jax.random.split(jax.random.key(seed), 10)
    fwd_tokens = bell_draw(streams_of[0], (SECTIONS, TOKENS, D), 1.0, 6.0, ((0, 4), (1, 8)))
    fwd_routes_keys = jax.random.split(jax.random.fold_in(streams_of[1], 1), SECTIONS * TOKENS // TOK_DEV)
    fwd_routes_turns = jax.random.permutation(jax.random.fold_in(streams_of[1], 3), SECTIONS * TOKENS // TOK_DEV)
    fwd_routes = jax.vmap(lambda own, number: routed_block(jax.random.fold_in(streams_of[1], 2), own, number, TOK_DEV, EXPERTS, TOP, CAP, 2))(fwd_routes_keys, fwd_routes_turns).reshape((SECTIONS, TOKENS, TOP))
    fwd_weights = jnp.clip(0.2 + 0.8 * jax.random.uniform(streams_of[2], (SECTIONS, TOKENS, TOP), jnp.float32) ** shard_levels(streams_of[2], (SECTIONS, TOKENS, TOP), ((0, 4), (1, 8)), -0.2, 0.2), 0.2, 1.0)
    bwd_tokens = bell_draw(streams_of[3], (SECTIONS, TOKENS, D), 1.0, 6.0, ((0, 4), (1, 8)))
    bwd_grads = bell_draw(streams_of[4], (SECTIONS, TOKENS, D), 1.0, 6.0, ((0, 4), (1, 8)))
    bwd_routes_keys = jax.random.split(jax.random.fold_in(streams_of[5], 1), SECTIONS * TOKENS // TOK_DEV)
    bwd_routes_turns = jax.random.permutation(jax.random.fold_in(streams_of[5], 3), SECTIONS * TOKENS // TOK_DEV)
    bwd_routes = jax.vmap(lambda own, number: routed_block(jax.random.fold_in(streams_of[5], 2), own, number, TOK_DEV, EXPERTS, TOP, CAP, 2))(bwd_routes_keys, bwd_routes_turns).reshape((SECTIONS, TOKENS, TOP))
    bwd_weights = jnp.clip(0.2 + 0.8 * jax.random.uniform(streams_of[6], (SECTIONS, TOKENS, TOP), jnp.float32) ** shard_levels(streams_of[6], (SECTIONS, TOKENS, TOP), ((0, 4), (1, 8)), -0.2, 0.2), 0.2, 1.0)
    up_proj = bell_draw(streams_of[7], (SECTIONS, D, EXPERTS * FF), D ** -0.5, 0.09375, ((0, 4), (2, 8)))
    down_proj = bell_draw(streams_of[8], (SECTIONS, EXPERTS * FF, D), FF ** -0.5, 0.1875, ((0, 4), (1, 8)))
    return {"fwd_tokens": fwd_tokens, "fwd_routes": fwd_routes, "fwd_weights": fwd_weights, "bwd_tokens": bwd_tokens, "bwd_grads": bwd_grads, "bwd_routes": bwd_routes, "bwd_weights": bwd_weights, "up_proj": up_proj, "down_proj": down_proj}


def silu_slope(pre_act):
    sigmoid_value = jax.nn.sigmoid(pre_act)
    return sigmoid_value * (1.0 + pre_act * (1.0 - sigmoid_value))


def slot_indices(routes):
    chosen = routes.reshape(N_EP, TOK_DEV * TOP)
    onehot = (chosen[:, :, None] == jnp.arange(EXPERTS, dtype=jnp.int32)[None, None, :]).astype(jnp.int32)
    earlier = jnp.cumsum(onehot, axis=1) - onehot
    position = jnp.sum(earlier * onehot, axis=2).astype(jnp.int32)
    source = jnp.broadcast_to(jnp.arange(N_EP, dtype=jnp.int32)[:, None], chosen.shape)
    return chosen.reshape(-1), source.reshape(-1), position.reshape(-1)


def scatter_rows(values, expert_ids, source, position):
    spread = jnp.broadcast_to(values[:, None, :], (TOKENS, TOP, D)).reshape(TOKENS * TOP, D)
    buffer = jnp.zeros((EXPERTS, N_EP, CAP, D), jnp.bfloat16)
    buffer = buffer.at[expert_ids, source, position].set(spread)
    return buffer.reshape(EXPERTS, N_EP * CAP, D)


def combine(residual, results, expert_ids, source, position, route_weights):
    picked = results.reshape(EXPERTS, N_EP, CAP, D)[expert_ids, source, position]
    picked = picked.reshape(TOKENS, TOP, D).astype(jnp.float32)
    combined = residual.astype(jnp.float32) + jnp.sum(route_weights[:, :, None] * picked, axis=1)
    return combined.astype(jnp.bfloat16)


def forward_expert(operands):
    rows_in, up_part, down_part = operands
    halves = []
    for half_index in range(2):
        hidden = jax.nn.silu(jnp.dot(rows_in, up_part[:, half_index], preferred_element_type=jnp.float32)).astype(jnp.bfloat16)
        halves.append(jnp.dot(hidden, down_part[half_index], preferred_element_type=jnp.float32).astype(jnp.bfloat16))
    return (halves[0].astype(jnp.float32) + halves[1].astype(jnp.float32)).astype(jnp.bfloat16)


def backward_expert(operands):
    rows_in, grad_rows, up_part, down_part = operands
    halves = []
    for half_index in range(2):
        pre_act = jnp.dot(rows_in, up_part[:, half_index], preferred_element_type=jnp.float32)
        upstream = lax.dot_general(grad_rows, down_part[half_index], (((1,), (1,)), ((), ())), preferred_element_type=jnp.float32)
        hidden_grad = (silu_slope(pre_act) * upstream).astype(jnp.bfloat16)
        halves.append(lax.dot_general(hidden_grad, up_part[:, half_index], (((1,), (1,)), ((), ())), preferred_element_type=jnp.float32).astype(jnp.bfloat16))
    return (halves[0].astype(jnp.float32) + halves[1].astype(jnp.float32)).astype(jnp.bfloat16)


def one_section(operands):
    fwd_tokens, fwd_routes, fwd_weights, bwd_tokens, bwd_grads, bwd_routes, bwd_weights, up_proj, down_proj = operands
    up_parts = jnp.transpose(up_proj.reshape(D, EXPERTS, 2, FF_DEV), (1, 0, 2, 3))
    down_parts = down_proj.reshape(EXPERTS, 2, FF_DEV, D)
    fwd_ids, fwd_source, fwd_position = slot_indices(fwd_routes)
    fwd_buffer = scatter_rows(fwd_tokens, fwd_ids, fwd_source, fwd_position)
    fwd_results = lax.map(forward_expert, (fwd_buffer, up_parts, down_parts))
    fwd_out = combine(fwd_tokens, fwd_results, fwd_ids, fwd_source, fwd_position, fwd_weights)
    bwd_ids, bwd_source, bwd_position = slot_indices(bwd_routes)
    bwd_buffer = scatter_rows(bwd_tokens, bwd_ids, bwd_source, bwd_position)
    grad_buffer = scatter_rows(bwd_grads, bwd_ids, bwd_source, bwd_position)
    bwd_results = lax.map(backward_expert, (bwd_buffer, grad_buffer, up_parts, down_parts))
    bwd_out = combine(bwd_grads, bwd_results, bwd_ids, bwd_source, bwd_position, bwd_weights)
    return fwd_out, bwd_out


def reference(fwd_tokens, fwd_routes, fwd_weights, bwd_tokens, bwd_grads, bwd_routes, bwd_weights, up_proj, down_proj):
    fwd_all, bwd_all = lax.map(one_section, (fwd_tokens, fwd_routes, fwd_weights, bwd_tokens, bwd_grads, bwd_routes, bwd_weights, up_proj, down_proj))
    next_input = jnp.roll(fwd_all, 1, axis=0)
    prev_grad = jnp.roll(bwd_all, -1, axis=0)
    return (next_input, prev_grad)
```

```python
import functools

import jax
import jax.numpy as jnp
from jax import lax
from jax.experimental import pallas as pl
from jax.experimental.pallas import tpu as pltpu
from jax.sharding import PartitionSpec as P

MESH = pl.DeviceIdType.MESH
NT = (((1,), (1,)), ((), ()))
NN = (((1,), (0,)), ((), ()))


def from_behind(value, axis, by):
    size = lax.axis_size(axis)
    return lax.ppermute(value, axis, [(i, (i + by) % size) for i in range(size)])


def silu_slope(pre_act):
    sigmoid_value = jax.nn.sigmoid(pre_act)
    return sigmoid_value * (1.0 + pre_act * (1.0 - sigmoid_value))


def slot_numbers(routes, expert_count, capacity):
    chosen = routes[0]
    tok_rows, route_count = chosen.shape
    onehot = (
        chosen[:, :, None] == jnp.arange(expert_count, dtype=jnp.int32)[None, None, :]
    ).astype(jnp.int32)
    flat_hot = onehot.reshape(tok_rows * route_count, expert_count)
    earlier = jnp.cumsum(flat_hot, axis=0) - flat_hot
    position = jnp.sum(earlier * flat_hot, axis=1).reshape(tok_rows, route_count)
    return chosen * capacity + position


def pack_rows(sources, slots, slot_total):
    slot_table = jnp.sum(
        (slots[:, :, None] == jnp.arange(slot_total, dtype=jnp.int32)[None, None, :]).astype(
            jnp.bfloat16
        ),
        axis=1,
    )
    return tuple(
        lax.dot_general(
            slot_table, member, (((0,), (0,)), ((), ())), preferred_element_type=jnp.float32
        ).astype(jnp.bfloat16)
        for member in sources
    )


def combine_rows(residual, results, slots, route_weights):
    slot_total = results.shape[0]
    hot = slots[:, :, None] == jnp.arange(slot_total, dtype=jnp.int32)[None, None, :]
    table = jnp.sum(jnp.where(hot, route_weights[:, :, None], 0.0), axis=1)
    high = lax.reduce_precision(table, 8, 7)
    both = jnp.concatenate([high.astype(jnp.bfloat16), (table - high).astype(jnp.bfloat16)], axis=0)
    sums = jnp.dot(both, results, preferred_element_type=jnp.float32)
    rows = residual.shape[0]
    return (residual.astype(jnp.float32) + sums[:rows] + sums[rows:]).astype(jnp.bfloat16)


def relay_kernel(
    experts, f_in, x_in, g_in, up_ref, down_ref, f_out, b_out,
    f_rows, x_rows, g_rows, f_part, b_part, f_other, b_other,
    z_send, z_recv, l_sem, x_send, x_recv, xr_send, xr_recv, zr_send, zr_recv, lr_sem,
):
    me = lax.axis_index("ep")
    mine = me // 2
    half = lax.rem(me, 2)
    partner = 2 * mine + 1 - half
    capacity, width = f_in.shape[1], f_in.shape[2]
    piece = 512 if width % 512 == 0 else 128
    pieces = width // piece
    hidden_size = up_ref.shape[1]

    def ahead(k):
        return lax.rem(mine + k, experts)

    def behind(k):
        return lax.rem(mine + experts - k, experts)

    barrier = pltpu.get_barrier_semaphore()
    pl.semaphore_signal(barrier, inc=1, device_id={"ep": partner}, device_id_type=MESH)
    for k in range(1, experts):
        pl.semaphore_signal(
            barrier, inc=1, device_id={"ep": 2 * ahead(k) + half}, device_id_type=MESH
        )
    pl.semaphore_wait(barrier, experts)

    ins = (f_in, x_in, g_in)
    rows = (f_rows, x_rows, g_rows)
    parts = (f_part, b_part)
    others = (f_other, b_other)
    outs = (f_out, b_out)

    def along(a, k):
        return pltpu.make_async_remote_copy(
            src_ref=ins[a].at[ahead(k)], dst_ref=rows[a].at[k, 0],
            send_sem=z_send.at[a, k], recv_sem=z_recv.at[a, k],
            device_id={"ep": 2 * ahead(k) + half}, device_id_type=MESH,
        )

    def own(a):
        return pltpu.make_async_copy(ins[a].at[mine], rows[a].at[0, 0], l_sem.at[a])

    def across(a, k):
        return pltpu.make_async_remote_copy(
            src_ref=ins[a].at[mine] if k == 0 else rows[a].at[k, 0], dst_ref=rows[a].at[k, 1],
            send_sem=x_send.at[a, k], recv_sem=x_recv.at[a, k],
            device_id={"ep": partner}, device_id_type=MESH,
        )

    def back_across(a, k):
        return pltpu.make_async_remote_copy(
            src_ref=parts[a].at[k, 1], dst_ref=others[a].at[k],
            send_sem=xr_send.at[a, k], recv_sem=xr_recv.at[a, k],
            device_id={"ep": partner}, device_id_type=MESH,
        )

    def back_along(a, k):
        return pltpu.make_async_remote_copy(
            src_ref=parts[a].at[k, 0], dst_ref=outs[a].at[mine],
            send_sem=zr_send.at[a, k], recv_sem=zr_recv.at[a, k],
            device_id={"ep": 2 * behind(k) + half}, device_id_type=MESH,
        )

    def back_own(a):
        return pltpu.make_async_copy(parts[a].at[0, 0], outs[a].at[mine], lr_sem.at[a])

    def columns(c):
        return pl.ds(pl.multiple_of(c * piece, piece), piece)

    def tile(ref, k, c):
        return ref[k, :, :, columns(c)].reshape(2 * capacity, piece)

    def arrived(a, k):
        if k == 0:
            own(a).wait()
        across(a, k).wait_recv()

    zeros = jnp.zeros((2 * capacity, hidden_size), jnp.float32)

    def forward(k):
        arrived(0, k)

        def first(c, total):
            return total + jnp.dot(
                tile(f_rows, k, c), up_ref[columns(c), :], preferred_element_type=jnp.float32
            )

        pre = lax.fori_loop(0, pieces, first, zeros)
        hidden = (pre * jax.nn.sigmoid(pre)).astype(jnp.bfloat16)

        def second(c, carry):
            product = jnp.dot(hidden, down_ref[:, columns(c)], preferred_element_type=jnp.float32)
            f_part[k, :, :, columns(c)] = product.astype(jnp.bfloat16).reshape(2, capacity, piece)
            return carry

        lax.fori_loop(0, pieces, second, 0)

    def backward(k):
        arrived(1, k)
        arrived(2, k)

        def first(c, totals):
            pre, up = totals
            pre = pre + jnp.dot(
                tile(x_rows, k, c), up_ref[columns(c), :], preferred_element_type=jnp.float32
            )
            up = up + lax.dot_general(
                tile(g_rows, k, c), down_ref[:, columns(c)], NT, preferred_element_type=jnp.float32
            )
            return pre, up

        pre, up = lax.fori_loop(0, pieces, first, (zeros, zeros))
        hidden_grad = (silu_slope(pre) * up).astype(jnp.bfloat16)

        def second(c, carry):
            product = lax.dot_general(
                hidden_grad, up_ref[columns(c), :], NT, preferred_element_type=jnp.float32
            )
            b_part[k, :, :, columns(c)] = product.astype(jnp.bfloat16).reshape(2, capacity, piece)
            return carry

        lax.fori_loop(0, pieces, second, 0)

    def home(a, k):
        back_across(a, k).wait_recv()

        def add(c, carry):
            total = parts[a][k, 0, :, columns(c)].astype(jnp.float32) + others[a][
                k, :, columns(c)
            ].astype(jnp.float32)
            parts[a][k, 0, :, columns(c)] = total.astype(jnp.bfloat16)
            return carry

        lax.fori_loop(0, pieces, add, 0)
        if k == 0:
            back_own(a).start()
        else:
            back_along(a, k).start()

    across(0, 0).start()
    for k in range(1, experts):
        along(0, k).start()
    for a in (1, 2):
        across(a, 0).start()
    for k in range(1, experts):
        for a in (1, 2):
            along(a, k).start()
    for a in range(3):
        own(a).start()

    for k in range(1, experts):
        along(0, k).wait_recv()
        across(0, k).start()
    for k in range(1, experts):
        for a in (1, 2):
            along(a, k).wait_recv()
            across(a, k).start()
        forward(k - 1)
        if k > 1:
            back_across(0, k - 1).start()
    forward(experts - 1)
    back_across(0, experts - 1).start()
    back_across(0, 0).start()
    backward(0)
    for k in range(1, experts):
        backward(k)
        back_across(1, k).start()
        home(0, k)
    back_across(1, 0).start()
    home(0, 0)
    for k in range(1, experts):
        home(1, k)
    home(1, 0)

    for a in range(2):
        back_own(a).wait()
        for k in range(1, experts):
            back_along(a, k).wait()
        for k in range(experts):
            back_across(a, k).wait_send()
    for a in range(3):
        for k in range(1, experts):
            along(a, k).wait_send()
        for k in range(experts):
            across(a, k).wait_send()


def relay(f_in, x_in, g_in, w_up, w_down):
    experts, capacity, width = f_in.shape
    hidden_size = w_up.shape[1]
    kept = jnp.bfloat16
    any_space = pl.BlockSpec(memory_space=pl.ANY)
    vmem = pl.BlockSpec(memory_space=pltpu.VMEM)
    received = pltpu.VMEM((experts, 2, capacity, width), kept)
    exchanged = pltpu.VMEM((experts, capacity, width), kept)
    dma = pltpu.SemaphoreType.DMA
    row_count = 2 * experts * capacity
    result = jax.ShapeDtypeStruct((experts, capacity, width), kept)
    return pl.pallas_call(
        functools.partial(relay_kernel, experts),
        out_shape=(result, result),
        in_specs=[any_space] * 3 + [vmem] * 2,
        out_specs=(any_space, any_space),
        scratch_shapes=[received] * 5 + [exchanged] * 2 + [
            dma((3, experts)), dma((3, experts)), dma((3,)),
            dma((3, experts)), dma((3, experts)),
            dma((2, experts)), dma((2, experts)),
            dma((2, experts)), dma((2, experts)), dma((2,)),
        ],
        compiler_params=pltpu.CompilerParams(
            collective_id=0, has_side_effects=True, vmem_limit_bytes=60 * 1024 * 1024
        ),
        cost_estimate=pl.CostEstimate(
            flops=10 * row_count * width * hidden_size,
            bytes_accessed=10 * row_count * width,
            transcendentals=2 * row_count * hidden_size,
        ),
    )(f_in, x_in, g_in, w_up, w_down)


def on_device(
    fwd_tokens,
    fwd_routes,
    fwd_weights,
    bwd_tokens,
    bwd_grads,
    bwd_routes,
    bwd_weights,
    up_proj,
    down_proj,
):
    ep_count = lax.axis_size("ep")
    expert_count = ep_count // 2
    tok_rows = fwd_tokens.shape[1]
    feature_count = fwd_tokens.shape[2]
    route_count = fwd_routes.shape[2]
    capacity = 3 * tok_rows * route_count // ep_count
    slot_total = expert_count * capacity
    fwd_slots = slot_numbers(fwd_routes, expert_count, capacity)
    bwd_slots = slot_numbers(bwd_routes, expert_count, capacity)
    packed = pack_rows((fwd_tokens[0],), fwd_slots, slot_total) + pack_rows(
        (bwd_tokens[0], bwd_grads[0]), bwd_slots, slot_total
    )
    packed = [member.reshape(expert_count, capacity, feature_count) for member in packed]
    fwd_results, bwd_results = relay(*packed, up_proj[0], down_proj[0])
    fwd_out = combine_rows(
        fwd_tokens[0], fwd_results.reshape(slot_total, feature_count), fwd_slots, fwd_weights[0]
    )
    bwd_out = combine_rows(
        bwd_grads[0], bwd_results.reshape(slot_total, feature_count), bwd_slots, bwd_weights[0]
    )
    next_input = from_behind(fwd_out[None], "pp", 1)
    prev_grad = from_behind(bwd_out[None], "pp", -1)
    return (next_input, prev_grad)


def solution(mesh):
    placed = (
        P("pp", "ep", None),
        P("pp", "ep", None),
        P("pp", "ep", None),
        P("pp", "ep", None),
        P("pp", "ep", None),
        P("pp", "ep", None),
        P("pp", "ep", None),
        P("pp", None, "ep"),
        P("pp", "ep", None),
    )
    return jax.shard_map(
        on_device,
        mesh=mesh,
        in_specs=placed,
        out_specs=(P("pp", "ep", None), P("pp", "ep", None)),
        check_vma=False,
    )
```

```python
import functools

import jax
import jax.numpy as jnp
from jax import lax
from jax.experimental import pallas as pl
from jax.experimental.pallas import tpu as pltpu
from jax.sharding import PartitionSpec as P

MESH = pl.DeviceIdType.MESH
NT = (((1,), (1,)), ((), ()))
NN = (((1,), (0,)), ((), ()))


def from_behind(value, axis, by):
    size = lax.axis_size(axis)
    return lax.ppermute(value, axis, [(i, (i + by) % size) for i in range(size)])


def silu_slope(pre_act):
    sigmoid_value = jax.nn.sigmoid(pre_act)
    return sigmoid_value * (1.0 + pre_act * (1.0 - sigmoid_value))


def slot_numbers(routes, expert_count, capacity):
    chosen = routes[0]
    tok_rows, route_count = chosen.shape
    onehot = (
        chosen[:, :, None] == jnp.arange(expert_count, dtype=jnp.int32)[None, None, :]
    ).astype(jnp.int32)
    flat_hot = onehot.reshape(tok_rows * route_count, expert_count)
    earlier = jnp.cumsum(flat_hot, axis=0) - flat_hot
    position = jnp.sum(earlier * flat_hot, axis=1).reshape(tok_rows, route_count)
    return chosen * capacity + position


def pack_rows(sources, slots, slot_total):
    slot_table = jnp.sum(
        (slots[:, :, None] == jnp.arange(slot_total, dtype=jnp.int32)[None, None, :]).astype(
            jnp.bfloat16
        ),
        axis=1,
    )
    return tuple(
        lax.dot_general(
            slot_table, member, (((0,), (0,)), ((), ())), preferred_element_type=jnp.float32
        ).astype(jnp.bfloat16)
        for member in sources
    )


def combine_rows(residual, results, slots, route_weights):
    slot_total = results.shape[0]
    hot = slots[:, :, None] == jnp.arange(slot_total, dtype=jnp.int32)[None, None, :]
    table = jnp.sum(jnp.where(hot, route_weights[:, :, None], 0.0), axis=1)
    high = lax.reduce_precision(table, 8, 7)
    both = jnp.concatenate([high.astype(jnp.bfloat16), (table - high).astype(jnp.bfloat16)], axis=0)
    sums = jnp.dot(both, results, preferred_element_type=jnp.float32)
    rows = residual.shape[0]
    return (residual.astype(jnp.float32) + sums[:rows] + sums[rows:]).astype(jnp.bfloat16)


def relay_kernel(
    experts, f_in, x_in, g_in, up_ref, down_ref, f_out, b_out,
    f_rows, x_rows, g_rows, f_part, b_part, f_other, b_other,
    z_send, z_recv, l_sem, x_send, x_recv, xr_send, xr_recv, zr_send, zr_recv, lr_sem,
):
    me = lax.axis_index("ep")
    mine = me // 2
    half = lax.rem(me, 2)
    partner = 2 * mine + 1 - half
    capacity, width = f_in.shape[1], f_in.shape[2]
    piece = 512 if width % 512 == 0 else 128
    pieces = width // piece
    hidden_size = up_ref.shape[1]

    def ahead(k):
        return lax.rem(mine + k, experts)

    def behind(k):
        return lax.rem(mine + experts - k, experts)

    barrier = pltpu.get_barrier_semaphore()
    pl.semaphore_signal(barrier, inc=1, device_id={"ep": partner}, device_id_type=MESH)
    for k in range(1, experts):
        pl.semaphore_signal(
            barrier, inc=1, device_id={"ep": 2 * ahead(k) + half}, device_id_type=MESH
        )
    pl.semaphore_wait(barrier, experts)

    ins = (f_in, x_in, g_in)
    rows = (f_rows, x_rows, g_rows)
    parts = (f_part, b_part)
    others = (f_other, b_other)
    outs = (f_out, b_out)

    def along(a, k):
        return pltpu.make_async_remote_copy(
            src_ref=ins[a].at[ahead(k)], dst_ref=rows[a].at[k, 0],
            send_sem=z_send.at[a, k], recv_sem=z_recv.at[a, k],
            device_id={"ep": 2 * ahead(k) + half}, device_id_type=MESH,
        )

    def own(a):
        return pltpu.make_async_copy(ins[a].at[mine], rows[a].at[0, 0], l_sem.at[a])

    def across(a, k):
        return pltpu.make_async_remote_copy(
            src_ref=ins[a].at[mine] if k == 0 else rows[a].at[k, 0], dst_ref=rows[a].at[k, 1],
            send_sem=x_send.at[a, k], recv_sem=x_recv.at[a, k],
            device_id={"ep": partner}, device_id_type=MESH,
        )

    def back_across(a, k):
        return pltpu.make_async_remote_copy(
            src_ref=parts[a].at[k, 1], dst_ref=others[a].at[k],
            send_sem=xr_send.at[a, k], recv_sem=xr_recv.at[a, k],
            device_id={"ep": partner}, device_id_type=MESH,
        )

    def back_along(a, k):
        return pltpu.make_async_remote_copy(
            src_ref=parts[a].at[k, 0], dst_ref=outs[a].at[mine],
            send_sem=zr_send.at[a, k], recv_sem=zr_recv.at[a, k],
            device_id={"ep": 2 * behind(k) + half}, device_id_type=MESH,
        )

    def back_own(a):
        return pltpu.make_async_copy(parts[a].at[0, 0], outs[a].at[mine], lr_sem.at[a])

    def columns(c):
        return pl.ds(pl.multiple_of(c * piece, piece), piece)

    def tile(ref, k, c):
        return ref[k, :, :, columns(c)].reshape(2 * capacity, piece)

    def arrived(a, k):
        if k == 0:
            own(a).wait()
        across(a, k).wait_recv()

    zeros = jnp.zeros((2 * capacity, hidden_size), jnp.float32)

    def forward(k):
        arrived(0, k)

        def first(c, total):
            return total + jnp.dot(
                tile(f_rows, k, c), up_ref[columns(c), :], preferred_element_type=jnp.float32
            )

        pre = lax.fori_loop(0, pieces, first, zeros)
        hidden = (pre * jax.nn.sigmoid(pre)).astype(jnp.bfloat16)

        def second(c, carry):
            product = jnp.dot(hidden, down_ref[:, columns(c)], preferred_element_type=jnp.float32)
            f_part[k, :, :, columns(c)] = product.astype(jnp.bfloat16).reshape(2, capacity, piece)
            return carry

        lax.fori_loop(0, pieces, second, 0)

    def backward(k):
        arrived(1, k)
        arrived(2, k)

        def first(c, totals):
            pre, up = totals
            pre = pre + jnp.dot(
                tile(x_rows, k, c), up_ref[columns(c), :], preferred_element_type=jnp.float32
            )
            up = up + lax.dot_general(
                tile(g_rows, k, c), down_ref[:, columns(c)], NT, preferred_element_type=jnp.float32
            )
            return pre, up

        pre, up = lax.fori_loop(0, pieces, first, (zeros, zeros))
        hidden_grad = (silu_slope(pre) * up).astype(jnp.bfloat16)

        def second(c, carry):
            product = lax.dot_general(
                hidden_grad, up_ref[columns(c), :], NT, preferred_element_type=jnp.float32
            )
            b_part[k, :, :, columns(c)] = product.astype(jnp.bfloat16).reshape(2, capacity, piece)
            return carry

        lax.fori_loop(0, pieces, second, 0)

    def home(a, k):
        back_across(a, k).wait_recv()

        def add(c, carry):
            total = parts[a][k, 0, :, columns(c)].astype(jnp.float32) + others[a][
                k, :, columns(c)
            ].astype(jnp.float32)
            parts[a][k, 0, :, columns(c)] = total.astype(jnp.bfloat16)
            return carry

        lax.fori_loop(0, pieces, add, 0)
        if k == 0:
            back_own(a).start()
        else:
            back_along(a, k).start()

    across(0, 0).start()
    for k in range(1, experts):
        along(0, k).start()
    for a in range(3):
        own(a).start()
    for a in (1, 2):
        across(a, 0).start()

    for k in range(1, experts):
        along(0, k).wait_recv()
        across(0, k).start()
        along(1, k).start()
    forward(0)
    for k in range(1, experts):
        along(1, k).wait_recv()
        across(1, k).start()
        along(2, k).start()
        forward(k)
        back_across(0, k).start()
    for k in range(1, experts):
        along(2, k).wait_recv()
        across(2, k).start()
        home(0, k)
    back_across(0, 0).start()
    backward(0)
    for k in range(1, experts):
        backward(k)
        back_across(1, k).start()
        if k > 1:
            home(1, k - 1)
    back_across(1, 0).start()
    home(0, 0)
    home(1, experts - 1)
    home(1, 0)

    for a in range(2):
        back_own(a).wait()
        for k in range(1, experts):
            back_along(a, k).wait()
        for k in range(experts):
            back_across(a, k).wait_send()
    for a in range(3):
        for k in range(1, experts):
            along(a, k).wait_send()
        for k in range(experts):
            across(a, k).wait_send()


def relay(f_in, x_in, g_in, w_up, w_down):
    experts, capacity, width = f_in.shape
    hidden_size = w_up.shape[1]
    kept = jnp.bfloat16
    any_space = pl.BlockSpec(memory_space=pl.ANY)
    vmem = pl.BlockSpec(memory_space=pltpu.VMEM)
    received = pltpu.VMEM((experts, 2, capacity, width), kept)
    exchanged = pltpu.VMEM((experts, capacity, width), kept)
    dma = pltpu.SemaphoreType.DMA
    row_count = 2 * experts * capacity
    result = jax.ShapeDtypeStruct((experts, capacity, width), kept)
    return pl.pallas_call(
        functools.partial(relay_kernel, experts),
        out_shape=(result, result),
        in_specs=[any_space] * 3 + [vmem] * 2,
        out_specs=(any_space, any_space),
        scratch_shapes=[received] * 5 + [exchanged] * 2 + [
            dma((3, experts)), dma((3, experts)), dma((3,)),
            dma((3, experts)), dma((3, experts)),
            dma((2, experts)), dma((2, experts)),
            dma((2, experts)), dma((2, experts)), dma((2,)),
        ],
        compiler_params=pltpu.CompilerParams(
            collective_id=0, has_side_effects=True, vmem_limit_bytes=60 * 1024 * 1024
        ),
        cost_estimate=pl.CostEstimate(
            flops=10 * row_count * width * hidden_size,
            bytes_accessed=10 * row_count * width,
            transcendentals=2 * row_count * hidden_size,
        ),
    )(f_in, x_in, g_in, w_up, w_down)


def on_device(
    fwd_tokens,
    fwd_routes,
    fwd_weights,
    bwd_tokens,
    bwd_grads,
    bwd_routes,
    bwd_weights,
    up_proj,
    down_proj,
):
    ep_count = lax.axis_size("ep")
    expert_count = ep_count // 2
    tok_rows = fwd_tokens.shape[1]
    feature_count = fwd_tokens.shape[2]
    route_count = fwd_routes.shape[2]
    capacity = 3 * tok_rows * route_count // ep_count
    slot_total = expert_count * capacity
    fwd_slots = slot_numbers(fwd_routes, expert_count, capacity)
    bwd_slots = slot_numbers(bwd_routes, expert_count, capacity)
    packed = pack_rows((fwd_tokens[0],), fwd_slots, slot_total) + pack_rows(
        (bwd_tokens[0], bwd_grads[0]), bwd_slots, slot_total
    )
    packed = [member.reshape(expert_count, capacity, feature_count) for member in packed]
    fwd_results, bwd_results = relay(*packed, up_proj[0], down_proj[0])
    fwd_out = combine_rows(
        fwd_tokens[0], fwd_results.reshape(slot_total, feature_count), fwd_slots, fwd_weights[0]
    )
    bwd_out = combine_rows(
        bwd_grads[0], bwd_results.reshape(slot_total, feature_count), bwd_slots, bwd_weights[0]
    )
    next_input = from_behind(fwd_out[None], "pp", 1)
    prev_grad = from_behind(bwd_out[None], "pp", -1)
    return (next_input, prev_grad)


def solution(mesh):
    placed = (
        P("pp", "ep", None),
        P("pp", "ep", None),
        P("pp", "ep", None),
        P("pp", "ep", None),
        P("pp", "ep", None),
        P("pp", "ep", None),
        P("pp", "ep", None),
        P("pp", None, "ep"),
        P("pp", "ep", None),
    )
    return jax.shard_map(
        on_device,
        mesh=mesh,
        in_specs=placed,
        out_specs=(P("pp", "ep", None), P("pp", "ep", None)),
        check_vma=False,
    )
```

```python
import functools

import jax
import jax.numpy as jnp
from jax import lax
from jax.experimental import pallas as pl
from jax.experimental.pallas import tpu as pltpu
from jax.sharding import PartitionSpec as P

MESH = pl.DeviceIdType.MESH
NT = (((1,), (1,)), ((), ()))
NN = (((1,), (0,)), ((), ()))


def silu_slope(pre_act):
    sigmoid_value = jax.nn.sigmoid(pre_act)
    return sigmoid_value * (1.0 + pre_act * (1.0 - sigmoid_value))


def slot_numbers(chosen, expert_count, capacity):
    batch, tok_rows, route_count = chosen.shape
    flat = chosen.reshape(batch, tok_rows * route_count)
    hot = flat[:, :, None] == jnp.arange(expert_count, dtype=jnp.int32)
    order = jnp.arange(tok_rows * route_count, dtype=jnp.int32)
    before = (order[None, :] < order[:, None]).astype(jnp.bfloat16)
    earlier = jnp.einsum(
        "ij,bje->bie", before, hot.astype(jnp.bfloat16), preferred_element_type=jnp.float32
    )
    position = jnp.sum(jnp.where(hot, earlier, 0.0), axis=2).astype(jnp.int32)
    return chosen * capacity + position.reshape(chosen.shape)


def pick_table(slots, expert_count, capacity):
    batch, tok_rows, _ = slots.shape
    numbers = jnp.arange(expert_count * capacity, dtype=jnp.int32)[None, :, None]
    first, second = slots[:, None, :, 0], slots[:, None, :, 1]
    table = ((numbers == first) | (numbers == second)).astype(jnp.bfloat16)
    return table.reshape(batch, expert_count, capacity, tok_rows)


def weigh_table(slots, route_weights, slot_total):
    hot = slots[:, :, :, None] == jnp.arange(slot_total, dtype=jnp.int32)
    table = jnp.sum(jnp.where(hot, route_weights[:, :, :, None], 0.0), axis=2)
    high = lax.reduce_precision(table, 8, 7)
    return jnp.concatenate([high.astype(jnp.bfloat16), (table - high).astype(jnp.bfloat16)], axis=1)


def relay_kernel(
    experts, sections, f_tok, x_tok, g_tok, pick_ref, weigh_ref, up_ref, down_ref, next_ref, prev_ref,
    f_rows, x_rows, g_rows, f_part, b_part, f_other, b_other, f_out, b_out, f_final, b_final,
    z_send, z_recv, x_send, x_recv, xr_send, xr_recv, zr_send, zr_recv, lr_sem, p_send, p_recv,
):
    me = lax.axis_index("ep")
    mine = me // 2
    half = lax.rem(me, 2)
    partner = 2 * mine + 1 - half
    section = lax.axis_index("pp")
    targets = (lax.rem(section + 1, sections), lax.rem(section + sections - 1, sections))
    capacity, width = f_rows.shape[2], f_rows.shape[3]
    tok_rows = f_tok.shape[0]
    piece = 512 if width % 512 == 0 else 128
    pieces = width // piece
    hidden_size = up_ref.shape[1]

    def ahead(k):
        return lax.rem(mine + k, experts)

    def behind(k):
        return lax.rem(mine + experts - k, experts)

    barrier = pltpu.get_barrier_semaphore()
    pl.semaphore_signal(barrier, inc=1, device_id={"ep": partner}, device_id_type=MESH)
    for k in range(1, experts):
        pl.semaphore_signal(
            barrier, inc=1, device_id={"ep": 2 * ahead(k) + half}, device_id_type=MESH
        )
    for target in targets:
        pl.semaphore_signal(barrier, inc=1, device_id={"pp": target}, device_id_type=MESH)
    pl.semaphore_wait(barrier, experts + 2)

    toks = (f_tok, x_tok, g_tok)
    rows = (f_rows, x_rows, g_rows)
    parts = (f_part, b_part)
    others = (f_other, b_other)
    outs = (f_out, b_out)
    finals = (f_final, b_final)
    ends = (next_ref, prev_ref)

    def staged(a, k):
        if k == 0:
            return rows[a].at[0, 0]
        return (f_part.at[k, 0], b_part.at[k, 0], b_part.at[k, 1])[a]

    def along(a, k):
        return pltpu.make_async_remote_copy(
            src_ref=staged(a, k), dst_ref=rows[a].at[k, 0],
            send_sem=z_send.at[a, k], recv_sem=z_recv.at[a, k],
            device_id={"ep": 2 * ahead(k) + half}, device_id_type=MESH,
        )

    def across(a, k):
        return pltpu.make_async_remote_copy(
            src_ref=rows[a].at[k, 0], dst_ref=rows[a].at[k, 1],
            send_sem=x_send.at[a, k], recv_sem=x_recv.at[a, k],
            device_id={"ep": partner}, device_id_type=MESH,
        )

    def back_across(a, k):
        return pltpu.make_async_remote_copy(
            src_ref=parts[a].at[k, 1], dst_ref=others[a].at[k],
            send_sem=xr_send.at[a, k], recv_sem=xr_recv.at[a, k],
            device_id={"ep": partner}, device_id_type=MESH,
        )

    def back_along(a, k):
        return pltpu.make_async_remote_copy(
            src_ref=parts[a].at[k, 0], dst_ref=outs[a].at[mine],
            send_sem=zr_send.at[a, k], recv_sem=zr_recv.at[a, k],
            device_id={"ep": 2 * behind(k) + half}, device_id_type=MESH,
        )

    def back_own(a):
        return pltpu.make_async_copy(parts[a].at[0, 0], outs[a].at[mine], lr_sem.at[a])

    def columns(c):
        return pl.ds(pl.multiple_of(c * piece, piece), piece)

    def tile(ref, k, c):
        return ref[k, :, :, columns(c)].reshape(2 * capacity, piece)

    def arrived(a, k):
        across(a, k).wait_recv()
        if k > 0:
            along(a, k).wait_send()

    def pack(a, k):
        table = pick_ref[min(a, 1), ahead(k)]
        place = staged(a, k)

        def put(c, carry):
            picked = jnp.dot(table, toks[a][:, columns(c)], preferred_element_type=jnp.float32)
            place[:, columns(c)] = picked.astype(jnp.bfloat16)
            return carry

        lax.fori_loop(0, pieces, put, 0)

    def relayed(a, c):
        place = pl.ds(c * piece, piece)
        return pltpu.make_async_remote_copy(
            src_ref=finals[a].at[:, place], dst_ref=ends[a].at[:, place],
            send_sem=p_send.at[a, c], recv_sem=p_recv.at[a, c],
            device_id={"pp": targets[a]}, device_id_type=MESH,
        )

    def combine(a):
        back_own(a).wait()
        for k in range(1, experts):
            back_along(a, k).wait_recv()
        residual = (f_tok, g_tok)[a]
        for c in range(pieces):
            place = pl.ds(c * piece, piece)
            results = outs[a][:, :, place].reshape(experts * capacity, piece)
            sums = jnp.dot(weigh_ref[a], results, preferred_element_type=jnp.float32)
            total = residual[:, place].astype(jnp.float32) + sums[:tok_rows] + sums[tok_rows:]
            finals[a][:, place] = total.astype(jnp.bfloat16)
            relayed(a, c).start()

    zeros = jnp.zeros((2 * capacity, hidden_size), jnp.float32)

    def forward(k):
        arrived(0, k)

        def first(c, total):
            return total + jnp.dot(
                tile(f_rows, k, c), up_ref[columns(c), :], preferred_element_type=jnp.float32
            )

        pre = lax.fori_loop(0, pieces, first, zeros)
        hidden = (pre * jax.nn.sigmoid(pre)).astype(jnp.bfloat16)

        def second(c, carry):
            product = jnp.dot(hidden, down_ref[:, columns(c)], preferred_element_type=jnp.float32)
            f_part[k, :, :, columns(c)] = product.astype(jnp.bfloat16).reshape(2, capacity, piece)
            return carry

        lax.fori_loop(0, pieces, second, 0)

    def backward(k):
        arrived(1, k)
        arrived(2, k)

        def first(c, totals):
            pre, up = totals
            pre = pre + jnp.dot(
                tile(x_rows, k, c), up_ref[columns(c), :], preferred_element_type=jnp.float32
            )
            up = up + lax.dot_general(
                tile(g_rows, k, c), down_ref[:, columns(c)], NT, preferred_element_type=jnp.float32
            )
            return pre, up

        pre, up = lax.fori_loop(0, pieces, first, (zeros, zeros))
        hidden_grad = (silu_slope(pre) * up).astype(jnp.bfloat16)

        def second(c, carry):
            product = lax.dot_general(
                hidden_grad, up_ref[columns(c), :], NT, preferred_element_type=jnp.float32
            )
            b_part[k, :, :, columns(c)] = product.astype(jnp.bfloat16).reshape(2, capacity, piece)
            return carry

        lax.fori_loop(0, pieces, second, 0)

    def home(a, k):
        back_across(a, k).wait_recv()

        def add(c, carry):
            total = parts[a][k, 0, :, columns(c)].astype(jnp.float32) + others[a][
                k, :, columns(c)
            ].astype(jnp.float32)
            parts[a][k, 0, :, columns(c)] = total.astype(jnp.bfloat16)
            return carry

        lax.fori_loop(0, pieces, add, 0)
        if k == 0:
            back_own(a).start()
        else:
            back_along(a, k).start()

    for k in range(1, experts):
        pack(0, k)
        along(0, k).start()
    for a in range(3):
        pack(a, 0)
        across(a, 0).start()
    for a in (1, 2):
        for k in range(1, experts):
            pack(a, k)

    for k in range(1, experts):
        along(0, k).wait_recv()
        across(0, k).start()
        along(1, k).start()
    forward(0)
    for k in range(1, experts):
        along(1, k).wait_recv()
        across(1, k).start()
        along(2, k).start()
        forward(k)
        back_across(0, k).start()
    for k in range(1, experts):
        along(2, k).wait_recv()
        across(2, k).start()
        home(0, k)
    back_across(0, 0).start()
    backward(0)
    for k in range(1, experts):
        backward(k)
        back_across(1, k).start()
        if k > 1:
            home(1, k - 1)
    back_across(1, 0).start()
    home(0, 0)
    combine(0)
    home(1, experts - 1)
    home(1, 0)
    combine(1)

    for a in range(2):
        for k in range(1, experts):
            back_along(a, k).wait_send()
        for k in range(experts):
            back_across(a, k).wait_send()
    for a in range(3):
        for k in range(experts):
            across(a, k).wait_send()
    for a in range(2):
        for c in range(pieces):
            relayed(a, c).wait()


def relay(f_tok, x_tok, g_tok, pick, weigh, w_up, w_down):
    _, experts, capacity, tok_rows = pick.shape
    width = f_tok.shape[1]
    hidden_size = w_up.shape[1]
    sections = lax.axis_size("pp")
    kept = jnp.bfloat16
    any_space = pl.BlockSpec(memory_space=pl.ANY)
    vmem = pl.BlockSpec(memory_space=pltpu.VMEM)
    received = pltpu.VMEM((experts, 2, capacity, width), kept)
    exchanged = pltpu.VMEM((experts, capacity, width), kept)
    final = pltpu.VMEM((tok_rows, width), kept)
    dma = pltpu.SemaphoreType.DMA
    pieces = width // (512 if width % 512 == 0 else 128)
    row_count = 2 * experts * capacity
    result = jax.ShapeDtypeStruct((tok_rows, width), kept)
    return pl.pallas_call(
        functools.partial(relay_kernel, experts, sections),
        out_shape=(result, result),
        in_specs=[vmem] * 7,
        out_specs=(any_space, any_space),
        scratch_shapes=[received] * 5 + [exchanged] * 4 + [final] * 2 + [
            dma((3, experts)), dma((3, experts)),
            dma((3, experts)), dma((3, experts)),
            dma((2, experts)), dma((2, experts)),
            dma((2, experts)), dma((2, experts)), dma((2,)),
            dma((2, pieces)), dma((2, pieces)),
        ],
        compiler_params=pltpu.CompilerParams(
            collective_id=0, has_side_effects=True, vmem_limit_bytes=60 * 1024 * 1024
        ),
        cost_estimate=pl.CostEstimate(
            flops=10 * row_count * width * hidden_size,
            bytes_accessed=10 * row_count * width,
            transcendentals=2 * row_count * hidden_size,
        ),
    )(f_tok, x_tok, g_tok, pick, weigh, w_up, w_down)


def on_device(
    fwd_tokens,
    fwd_routes,
    fwd_weights,
    bwd_tokens,
    bwd_grads,
    bwd_routes,
    bwd_weights,
    up_proj,
    down_proj,
):
    ep_count = lax.axis_size("ep")
    expert_count = ep_count // 2
    tok_rows = fwd_tokens.shape[1]
    route_count = fwd_routes.shape[2]
    capacity = 3 * tok_rows * route_count // ep_count
    slot_total = expert_count * capacity
    slots = slot_numbers(jnp.concatenate([fwd_routes, bwd_routes]), expert_count, capacity)
    pick = pick_table(slots, expert_count, capacity)
    weigh = weigh_table(slots, jnp.concatenate([fwd_weights, bwd_weights]), slot_total)
    next_input, prev_grad = relay(
        fwd_tokens[0], bwd_tokens[0], bwd_grads[0], pick, weigh, up_proj[0], down_proj[0]
    )
    return (next_input[None], prev_grad[None])


def solution(mesh):
    placed = (
        P("pp", "ep", None),
        P("pp", "ep", None),
        P("pp", "ep", None),
        P("pp", "ep", None),
        P("pp", "ep", None),
        P("pp", "ep", None),
        P("pp", "ep", None),
        P("pp", None, "ep"),
        P("pp", "ep", None),
    )
    return jax.shard_map(
        on_device,
        mesh=mesh,
        in_specs=placed,
        out_specs=(P("pp", "ep", None), P("pp", "ep", None)),
        check_vma=False,
    )
```

```python
import functools

import jax
import jax.numpy as jnp
from jax import lax
from jax.experimental import pallas as pl
from jax.experimental.pallas import tpu as pltpu
from jax.sharding import PartitionSpec as P

MESH = pl.DeviceIdType.MESH
NT = (((1,), (1,)), ((), ()))
NN = (((1,), (0,)), ((), ()))


def silu_slope(pre_act):
    sigmoid_value = jax.nn.sigmoid(pre_act)
    return sigmoid_value * (1.0 + pre_act * (1.0 - sigmoid_value))


def slot_numbers(chosen, expert_count, capacity):
    batch, tok_rows, route_count = chosen.shape
    flat = chosen.reshape(batch, tok_rows * route_count)
    hot = flat[:, :, None] == jnp.arange(expert_count, dtype=jnp.int32)
    order = jnp.arange(tok_rows * route_count, dtype=jnp.int32)
    before = (order[None, :] < order[:, None]).astype(jnp.bfloat16)
    earlier = jnp.einsum(
        "ij,bje->bie", before, hot.astype(jnp.bfloat16), preferred_element_type=jnp.float32
    )
    position = jnp.sum(jnp.where(hot, earlier, 0.0), axis=2).astype(jnp.int32)
    return chosen * capacity + position.reshape(chosen.shape)


def pick_table(slots, expert_count, capacity):
    batch, tok_rows, _ = slots.shape
    numbers = jnp.arange(expert_count * capacity, dtype=jnp.int32)[None, :, None]
    first, second = slots[:, None, :, 0], slots[:, None, :, 1]
    table = ((numbers == first) | (numbers == second)).astype(jnp.bfloat16)
    return table.reshape(batch, expert_count, capacity, tok_rows)


def weigh_table(slots, route_weights, slot_total):
    hot = slots[:, :, :, None] == jnp.arange(slot_total, dtype=jnp.int32)
    table = jnp.sum(jnp.where(hot, route_weights[:, :, :, None], 0.0), axis=2)
    high = lax.reduce_precision(table, 8, 7)
    return jnp.concatenate([high.astype(jnp.bfloat16), (table - high).astype(jnp.bfloat16)], axis=1)


def relay_kernel(
    experts, sections, f_tok, x_tok, g_tok, pick_ref, weigh_ref, up_ref, down_ref, next_ref, prev_ref,
    f_rows, x_rows, g_rows, f_part, b_part, f_other, b_other, f_out, b_out, f_final, b_final,
    z_send, z_recv, x_send, x_recv, xr_send, xr_recv, zr_send, zr_recv, lr_sem, p_send, p_recv,
):
    me = lax.axis_index("ep")
    mine = me // 2
    half = lax.rem(me, 2)
    partner = 2 * mine + 1 - half
    section = lax.axis_index("pp")
    targets = (lax.rem(section + 1, sections), lax.rem(section + sections - 1, sections))
    capacity, width = f_rows.shape[2], f_rows.shape[3]
    tok_rows = f_tok.shape[0]
    piece = 512 if width % 512 == 0 else 128
    pieces = width // piece
    hidden_size = up_ref.shape[1]

    def ahead(k):
        return lax.rem(mine + k, experts)

    def behind(k):
        return lax.rem(mine + experts - k, experts)

    barrier = pltpu.get_barrier_semaphore()
    pl.semaphore_signal(barrier, inc=1, device_id={"ep": partner}, device_id_type=MESH)
    for k in range(1, experts):
        pl.semaphore_signal(
            barrier, inc=1, device_id={"ep": 2 * ahead(k) + half}, device_id_type=MESH
        )
    for target in targets:
        pl.semaphore_signal(barrier, inc=1, device_id={"pp": target}, device_id_type=MESH)
    pl.semaphore_wait(barrier, experts + 2)

    toks = (f_tok, x_tok, g_tok)
    rows = (f_rows, x_rows, g_rows)
    parts = (f_part, b_part)
    others = (f_other, b_other)
    outs = (f_out, b_out)
    finals = (f_final, b_final)
    ends = (next_ref, prev_ref)

    def staged(a, k):
        if k == 0:
            return rows[a].at[0, 0]
        return (f_part.at[k, 0], b_part.at[k, 0], b_part.at[k, 1])[a]

    def along(a, k):
        return pltpu.make_async_remote_copy(
            src_ref=staged(a, k), dst_ref=rows[a].at[k, 0],
            send_sem=z_send.at[a, k], recv_sem=z_recv.at[a, k],
            device_id={"ep": 2 * ahead(k) + half}, device_id_type=MESH,
        )

    def across(a, k):
        return pltpu.make_async_remote_copy(
            src_ref=rows[a].at[k, 0], dst_ref=rows[a].at[k, 1],
            send_sem=x_send.at[a, k], recv_sem=x_recv.at[a, k],
            device_id={"ep": partner}, device_id_type=MESH,
        )

    cuts = ((0, (pieces + 1) // 2), ((pieces + 1) // 2, pieces))

    def span(h):
        return pl.ds(cuts[h][0] * piece, (cuts[h][1] - cuts[h][0]) * piece)

    def back_across(a, k, h):
        return pltpu.make_async_remote_copy(
            src_ref=parts[a].at[k, 1, :, span(h)], dst_ref=others[a].at[k, :, span(h)],
            send_sem=xr_send.at[a, k, h], recv_sem=xr_recv.at[a, k, h],
            device_id={"ep": partner}, device_id_type=MESH,
        )

    def back_along(a, k, h):
        return pltpu.make_async_remote_copy(
            src_ref=parts[a].at[k, 0, :, span(h)], dst_ref=outs[a].at[mine, :, span(h)],
            send_sem=zr_send.at[a, k, h], recv_sem=zr_recv.at[a, k, h],
            device_id={"ep": 2 * behind(k) + half}, device_id_type=MESH,
        )

    def back_own(a, h):
        return pltpu.make_async_copy(
            parts[a].at[0, 0, :, span(h)], outs[a].at[mine, :, span(h)], lr_sem.at[a, h]
        )

    def columns(c):
        return pl.ds(pl.multiple_of(c * piece, piece), piece)

    def tile(ref, k, c):
        return ref[k, :, :, columns(c)].reshape(2 * capacity, piece)

    def arrived(a, k):
        across(a, k).wait_recv()
        if k > 0:
            along(a, k).wait_send()

    def pack(a, k):
        table = pick_ref[min(a, 1), ahead(k)]
        place = staged(a, k)

        def put(c, carry):
            picked = jnp.dot(table, toks[a][:, columns(c)], preferred_element_type=jnp.float32)
            place[:, columns(c)] = picked.astype(jnp.bfloat16)
            return carry

        lax.fori_loop(0, pieces, put, 0)

    def relayed(a, c):
        place = pl.ds(c * piece, piece)
        return pltpu.make_async_remote_copy(
            src_ref=finals[a].at[:, place], dst_ref=ends[a].at[:, place],
            send_sem=p_send.at[a, c], recv_sem=p_recv.at[a, c],
            device_id={"pp": targets[a]}, device_id_type=MESH,
        )

    def combine(a, h):
        back_own(a, h).wait()
        for k in range(1, experts):
            back_along(a, k, h).wait_recv()
        residual = (f_tok, g_tok)[a]
        for c in range(*cuts[h]):
            place = pl.ds(c * piece, piece)
            results = outs[a][:, :, place].reshape(experts * capacity, piece)
            sums = jnp.dot(weigh_ref[a], results, preferred_element_type=jnp.float32)
            total = residual[:, place].astype(jnp.float32) + sums[:tok_rows] + sums[tok_rows:]
            finals[a][:, place] = total.astype(jnp.bfloat16)
            relayed(a, c).start()

    zeros = jnp.zeros((2 * capacity, hidden_size), jnp.float32)

    def forward(k):
        arrived(0, k)

        def first(c, total):
            return total + jnp.dot(
                tile(f_rows, k, c), up_ref[columns(c), :], preferred_element_type=jnp.float32
            )

        pre = lax.fori_loop(0, pieces, first, zeros)
        hidden = (pre * jax.nn.sigmoid(pre)).astype(jnp.bfloat16)

        def second(c, carry):
            product = jnp.dot(hidden, down_ref[:, columns(c)], preferred_element_type=jnp.float32)
            f_part[k, :, :, columns(c)] = product.astype(jnp.bfloat16).reshape(2, capacity, piece)
            return carry

        lax.fori_loop(0, pieces, second, 0)

    def backward(k):
        arrived(1, k)
        arrived(2, k)

        def first(c, totals):
            pre, up = totals
            pre = pre + jnp.dot(
                tile(x_rows, k, c), up_ref[columns(c), :], preferred_element_type=jnp.float32
            )
            up = up + lax.dot_general(
                tile(g_rows, k, c), down_ref[:, columns(c)], NT, preferred_element_type=jnp.float32
            )
            return pre, up

        pre, up = lax.fori_loop(0, pieces, first, (zeros, zeros))
        hidden_grad = (silu_slope(pre) * up).astype(jnp.bfloat16)

        def second(c, carry):
            product = lax.dot_general(
                hidden_grad, up_ref[columns(c), :], NT, preferred_element_type=jnp.float32
            )
            b_part[k, :, :, columns(c)] = product.astype(jnp.bfloat16).reshape(2, capacity, piece)
            return carry

        lax.fori_loop(0, pieces, second, 0)

    def home(a, k, h):
        back_across(a, k, h).wait_recv()

        def add(c, carry):
            total = parts[a][k, 0, :, columns(c)].astype(jnp.float32) + others[a][
                k, :, columns(c)
            ].astype(jnp.float32)
            parts[a][k, 0, :, columns(c)] = total.astype(jnp.bfloat16)
            return carry

        lax.fori_loop(cuts[h][0], cuts[h][1], add, 0)
        if k == 0:
            back_own(a, h).start()
        else:
            back_along(a, k, h).start()

    for k in range(1, experts):
        pack(0, k)
        along(0, k).start()
    for a in range(3):
        pack(a, 0)
        across(a, 0).start()
    for a in (1, 2):
        for k in range(1, experts):
            pack(a, k)

    for k in range(1, experts):
        along(0, k).wait_recv()
        across(0, k).start()
        along(1, k).start()
    forward(0)
    for k in range(1, experts):
        along(1, k).wait_recv()
        across(1, k).start()
        along(2, k).start()
        forward(k)
        for h in range(2):
            back_across(0, k, h).start()
    for k in range(1, experts):
        along(2, k).wait_recv()
        across(2, k).start()
        for h in range(2):
            home(0, k, h)
    for h in range(2):
        back_across(0, 0, h).start()
    backward(0)
    for k in range(1, experts):
        backward(k)
        back_across(1, k, 0).start()
        if k > 1:
            home(1, k - 1, 0)
    back_across(1, 0, 0).start()
    back_across(1, 1, 1).start()
    for h in range(2):
        home(0, 0, h)
    for h in range(2):
        combine(0, h)
    for k in range(2, experts):
        back_across(1, k, 1).start()
    home(1, experts - 1, 0)
    home(1, 0, 0)
    back_across(1, 0, 1).start()
    home(1, 1, 1)
    combine(1, 0)
    for k in range(2, experts):
        home(1, k, 1)
    home(1, 0, 1)
    combine(1, 1)

    for a in range(2):
        for h in range(2):
            for k in range(1, experts):
                back_along(a, k, h).wait_send()
            for k in range(experts):
                back_across(a, k, h).wait_send()
    for a in range(3):
        for k in range(experts):
            across(a, k).wait_send()
    for a in range(2):
        for c in range(pieces):
            relayed(a, c).wait()


def relay(f_tok, x_tok, g_tok, pick, weigh, w_up, w_down):
    _, experts, capacity, tok_rows = pick.shape
    width = f_tok.shape[1]
    hidden_size = w_up.shape[1]
    sections = lax.axis_size("pp")
    kept = jnp.bfloat16
    any_space = pl.BlockSpec(memory_space=pl.ANY)
    vmem = pl.BlockSpec(memory_space=pltpu.VMEM)
    received = pltpu.VMEM((experts, 2, capacity, width), kept)
    exchanged = pltpu.VMEM((experts, capacity, width), kept)
    final = pltpu.VMEM((tok_rows, width), kept)
    dma = pltpu.SemaphoreType.DMA
    pieces = width // (512 if width % 512 == 0 else 128)
    row_count = 2 * experts * capacity
    result = jax.ShapeDtypeStruct((tok_rows, width), kept)
    return pl.pallas_call(
        functools.partial(relay_kernel, experts, sections),
        out_shape=(result, result),
        in_specs=[vmem] * 7,
        out_specs=(any_space, any_space),
        scratch_shapes=[received] * 5 + [exchanged] * 4 + [final] * 2 + [
            dma((3, experts)), dma((3, experts)),
            dma((3, experts)), dma((3, experts)),
            dma((2, experts, 2)), dma((2, experts, 2)),
            dma((2, experts, 2)), dma((2, experts, 2)), dma((2, 2)),
            dma((2, pieces)), dma((2, pieces)),
        ],
        compiler_params=pltpu.CompilerParams(
            collective_id=0, has_side_effects=True, vmem_limit_bytes=60 * 1024 * 1024
        ),
        cost_estimate=pl.CostEstimate(
            flops=10 * row_count * width * hidden_size,
            bytes_accessed=10 * row_count * width,
            transcendentals=2 * row_count * hidden_size,
        ),
    )(f_tok, x_tok, g_tok, pick, weigh, w_up, w_down)


def on_device(
    fwd_tokens,
    fwd_routes,
    fwd_weights,
    bwd_tokens,
    bwd_grads,
    bwd_routes,
    bwd_weights,
    up_proj,
    down_proj,
):
    ep_count = lax.axis_size("ep")
    expert_count = ep_count // 2
    tok_rows = fwd_tokens.shape[1]
    route_count = fwd_routes.shape[2]
    capacity = 3 * tok_rows * route_count // ep_count
    slot_total = expert_count * capacity
    slots = slot_numbers(jnp.concatenate([fwd_routes, bwd_routes]), expert_count, capacity)
    pick = pick_table(slots, expert_count, capacity)
    weigh = weigh_table(slots, jnp.concatenate([fwd_weights, bwd_weights]), slot_total)
    next_input, prev_grad = relay(
        fwd_tokens[0], bwd_tokens[0], bwd_grads[0], pick, weigh, up_proj[0], down_proj[0]
    )
    return (next_input[None], prev_grad[None])


def solution(mesh):
    placed = (
        P("pp", "ep", None),
        P("pp", "ep", None),
        P("pp", "ep", None),
        P("pp", "ep", None),
        P("pp", "ep", None),
        P("pp", "ep", None),
        P("pp", "ep", None),
        P("pp", None, "ep"),
        P("pp", "ep", None),
    )
    return jax.shard_map(
        on_device,
        mesh=mesh,
        in_specs=placed,
        out_specs=(P("pp", "ep", None), P("pp", "ep", None)),
        check_vma=False,
    )
```
